32 devices in a mesh: req: 16 (over z, y, core), tp: 2 (over x).
Axes of the slice: x: 2, y: 2, z: 4, core: 2. Of those that a mesh axis runs over, the one named last changes fastest.
Arguments:
- hidden: bfloat16 [64, 128, 2048], P('tp', 'req'), may hold values from -6 to 6
- norm_gain: float32 [2048], replicated, may hold values from 0.1 to 1.9
- w_query: bfloat16 [2048, 2048], P(None, 'tp'), may hold values from -0.45335272 to 0.45335272
- w_keyval: bfloat16 [2048, 4, 128], replicated, may hold values from -0.45335272 to 0.45335272
- w_out: bfloat16 [2048, 2048], P('tp'), may hold values from -0.25 to 0.25
- kv_pool: bfloat16 [1024, 256, 4, 128], P('req'), may hold values from -10 to 10
- cache_len: int32 [128], P('req'), may hold values from 1 to 4096, as said below
- draft_count: int32 [128], P('req'), may hold values from 32 to 64, as said below
- parents: int32 [128, 64], P('req'), may hold values from 0 to 62, as said below
Outputs:
- attended: bfloat16 [64, 128, 2048], P('tp', 'req')
The draws below stay inside these ranges and needn't reach their ends.
Inputs may be any that keep to these rules, and one draw needn't show every extreme that they name: `cache_len`: some request has exactly 4096. `draft_count`: some request has exactly 64. parents[r, t] < t for t >= 1 and parents[r, 0] = 0.
All inputs are finite; a program needn't handle non-finite values.
Results may differ from the reference program's by a relative error of at most 0.035.
Values may be sent and summed in bfloat16 or wider, within the bound.
A program may use at most 192 MiB of HBM per device.

```python
import math
import jax
import jax.numpy as jnp
from jax import lax

D = 2048
HQ = 32
HD = 64
KVH = 4
W = 2048
PAGE = 256
DRAFT = 64
MAXLEN = 4096
REQ_DEV = 8
REQUESTS = 128
PAGES = 8
POOL = 1024
CAP = 4
N_REQ = 16


def parent_table(key):
    upper = jnp.maximum(jnp.arange(DRAFT, dtype=jnp.int32), 1)
    upper = jnp.broadcast_to(upper[None, :], (REQUESTS, DRAFT))
    return jax.random.randint(jax.random.fold_in(key, 37), (REQUESTS, DRAFT), 0, upper, dtype=jnp.int32)


def draw_hidden(key, part):
    shape = (DRAFT, REQUESTS, D)
    values = jax.random.truncated_normal(jax.random.fold_in(key, 101), -6.0, 6.0, shape, jnp.float32)
    return values.astype(jnp.bfloat16)


def draw_w_query(key, part):
    values = jax.random.truncated_normal(jax.random.fold_in(key, 79), -6.0, 6.0, (D, HQ * HD), jnp.float32) * D ** (-0.5)
    return values.astype(jnp.bfloat16)


def draw_w_keyval(key, part):
    values = jax.random.truncated_normal(jax.random.fold_in(key, 83), -6.0, 6.0, (D, KVH, 2 * HD), jnp.float32) * D ** (-0.5)
    return values.astype(jnp.bfloat16)


def draw_kv_pool(key, part):
    first_key, second_key = jax.random.split(key, 2)
    shape = (POOL, PAGE, KVH, HD)
    keys = 2.0 * jax.random.truncated_normal(first_key, -5.0, 5.0, shape, jnp.float32)
    values = jax.random.truncated_normal(second_key, -5.0, 5.0, shape, jnp.float32)
    return jnp.concatenate([keys, values], axis=-1).astype(jnp.bfloat16)


def draw_cache_len(key, part):
    first_key, second_key = jax.random.split(jax.random.fold_in(key, 11), 2)
    lengths = jax.random.randint(first_key, (REQUESTS,), 1, MAXLEN + 1, dtype=jnp.int32)
    chosen = jax.random.randint(second_key, (), 0, REQUESTS, dtype=jnp.int32)
    return jnp.where(jnp.arange(REQUESTS, dtype=jnp.int32) == chosen, MAXLEN, lengths).astype(jnp.int32)


def draw_draft_count(key, part):
    first_key, second_key = jax.random.split(jax.random.fold_in(key, 23), 2)
    counts = jax.random.randint(first_key, (REQUESTS,), DRAFT // 2, DRAFT + 1, dtype=jnp.int32)
    chosen = jax.random.randint(second_key, (), 0, REQUESTS, dtype=jnp.int32)
    return jnp.where(jnp.arange(REQUESTS, dtype=jnp.int32) == chosen, DRAFT, counts).astype(jnp.int32)


def draw_parents(key, part):
    return parent_table(key)


def levels(rng, shape, shards, least, high):
    def one(dim, shards_of):
        draws = jax.random.uniform(jax.random.fold_in(jax.random.fold_in(rng, 6), dim), (shards_of,), jnp.float32, least / len(shards), high / len(shards))
        return jnp.repeat(jnp.exp(draws), shape[dim] // shards_of).reshape((-1,) + (1,) * (len(shape) - dim - 1))

    factor_of = one(*shards[0])
    for cut in shards[1:]:
        factor_of = factor_of * one(*cut)
    return factor_of


def noise(key, dims, deviation, most, pieces=(), kind=jnp.bfloat16):
    factor_of = levels(key, dims, pieces, -0.22, 0.18) if pieces else 1.0
    values = jax.random.normal(key, dims, jnp.float32) * deviation * factor_of
    return jnp.minimum(jnp.maximum(values, -most), most).astype(kind)


def setup_inputs(seed: int = 0) -> dict:
    key_of = jax.random.split(jax.random.key(seed), 10)
    return {
        "hidden": draw_hidden(jax.random.fold_in(key_of[9], 71), 0),
        "norm_gain": jnp.clip(1.0 + 0.18 * jax.random.normal(key_of[1], (D,), jnp.float32), 0.1, 1.9),
        "w_query": draw_w_query(jax.random.fold_in(key_of[9], 71), 0),
        "w_keyval": draw_w_keyval(jax.random.fold_in(key_of[9], 71), 0),
        "w_out": noise(key_of[4], (HQ * HD, D), (HQ * HD // 4) ** -0.5, 0.25, ((0, 2),)),
        "kv_pool": draw_kv_pool(jax.random.fold_in(key_of[9], 71), 0),
        "cache_len": draw_cache_len(jax.random.fold_in(key_of[9], 71), 0),
        "draft_count": draw_draft_count(jax.random.fold_in(key_of[9], 71), 0),
        "parents": draw_parents(jax.random.fold_in(key_of[9], 71), 0),
    }


eps = 1e-05
rope_base = 10000.0

def ancestry(parents):
    draft_len = parents.shape[-1]
    row_ids = lax.broadcasted_iota(jnp.int32, (draft_len, draft_len), 0)
    col_ids = lax.broadcasted_iota(jnp.int32, (draft_len, draft_len), 1)
    link_mask = jnp.logical_and(parents[..., :, None] == col_ids, row_ids > 0)
    reached = jnp.logical_or(link_mask, row_ids == col_ids).astype(jnp.float32)
    for doubling in range(max(1, (draft_len - 1).bit_length())):
        reached = (jnp.einsum('...ts,...su->...tu', reached, reached, precision=lax.Precision.HIGHEST) > 0.5).astype(jnp.float32)
    depths = (lax.optimization_barrier(jnp.sum(reached, axis=-1)) - 1.0).astype(jnp.int32)
    return (reached > 0.5, depths)

def rotate(vectors, position):
    half_dim = vectors.shape[-1] // 2
    frequency = jnp.exp(jnp.arange(half_dim, dtype=jnp.float32) * (-2.0 * math.log(rope_base) / vectors.shape[-1]))
    angles = position.astype(jnp.float32)[..., None, None] * frequency
    cos_part = jnp.cos(angles)
    sin_part = jnp.sin(angles)
    front_half = vectors[..., :half_dim]
    back_half = vectors[..., half_dim:]
    return jnp.concatenate([front_half * cos_part - back_half * sin_part, back_half * cos_part + front_half * sin_part], axis=-1)

def reference(hidden, norm_gain, w_query, w_keyval, w_out, kv_pool, cache_len, draft_count, parents):
    n_requests = hidden.shape[1]
    d_model = hidden.shape[2]
    inputs = hidden.astype(jnp.float32)
    normed = (inputs * lax.rsqrt(lax.optimization_barrier(jnp.mean(inputs * inputs, axis=-1, keepdims=True)) + eps) * norm_gain).astype(jnp.bfloat16)
    flattened = normed.reshape(-1, d_model)
    queries = jnp.dot(flattened, w_query, preferred_element_type=jnp.float32).reshape(DRAFT, n_requests, HQ, HD).transpose(1, 0, 2, 3)
    keyvals = jnp.dot(flattened, w_keyval.reshape(d_model, KVH * 2 * HD), preferred_element_type=jnp.float32)
    keyvals = keyvals.reshape(DRAFT, n_requests, KVH, 2 * HD).transpose(1, 0, 2, 3)
    reached, depths = ancestry(parents)
    position = cache_len[:, None] + depths
    queries = rotate(queries, position).astype(jnp.bfloat16)
    draft_kv = jnp.concatenate([rotate(keyvals[..., :HD], position), keyvals[..., HD:]], axis=-1).astype(jnp.bfloat16)
    first_slot = jnp.maximum(W - cache_len[:, None], depths + 1)
    req_ids = jnp.arange(n_requests, dtype=jnp.int32)
    home_group = req_ids // REQ_DEV
    local_slot = req_ids % REQ_DEV
    item_ids = local_slot[:, None] * PAGES + jnp.arange(PAGES, dtype=jnp.int32)[None, :]
    owner_ids = (home_group[:, None] + item_ids) % N_REQ
    page_index = (owner_ids * (REQ_DEV * PAGES) + home_group[:, None] * CAP + item_ids // N_REQ).astype(jnp.int32)

    def per_request(request_data):
        req_query, req_keys, req_reach, req_first, req_pages = request_data
        cache = kv_pool[req_pages].reshape(W, KVH, 2 * HD)
        all_keys = jnp.concatenate([cache, req_keys], axis=0).astype(jnp.float32)
        all_keys = jnp.repeat(all_keys, HQ // KVH, axis=1)
        slot_ids = jnp.arange(W, dtype=jnp.int32)
        visible = jnp.concatenate([slot_ids[None, :] >= req_first[:, None], req_reach], axis=1)
        scores = jnp.einsum('thd,jhd->thj', req_query.astype(jnp.float32), all_keys[..., :HD]) * HD ** (-0.5)
        keep_mask = visible[:, None, :]
        scores = jnp.where(keep_mask, scores, -1e+30)
        top_score = lax.optimization_barrier(jnp.max(scores, axis=-1, keepdims=True))
        weights = jnp.where(keep_mask, jnp.exp(scores - top_score), 0.0).astype(jnp.bfloat16)
        totals = lax.optimization_barrier(jnp.sum(weights.astype(jnp.float32), axis=-1))
        mixed = jnp.einsum('thj,jhd->thd', weights.astype(jnp.float32), all_keys[..., HD:]) / totals[..., None]
        return mixed.reshape(DRAFT, HQ * HD).astype(jnp.bfloat16)
    mixed_all = lax.map(per_request, (queries, draft_kv, reached, first_slot, page_index))
    projected = jnp.dot(mixed_all.transpose(1, 0, 2).reshape(-1, HQ * HD), w_out, preferred_element_type=jnp.float32)
    projected = projected.reshape(DRAFT, n_requests, d_model)
    valid_rows = jnp.arange(DRAFT, dtype=jnp.int32)[:, None] < draft_count[None, :]
    return jnp.where(valid_rows[..., None], projected, 0.0).astype(jnp.bfloat16)
```

```python
import functools
import math

import jax
import jax.numpy as jnp
from jax import lax
from jax.experimental import pallas as pl
from jax.experimental.pallas import tpu as pltpu
from jax.sharding import PartitionSpec as P

HQ = 32
KVH = 4
W = 2048


eps = 1e-05
rope_base = 10000.0
hidden_score = -1e30


def ancestry(parents):
    draft_len = parents.shape[-1]
    row_ids = lax.broadcasted_iota(jnp.int32, (draft_len, draft_len), 0)
    col_ids = lax.broadcasted_iota(jnp.int32, (draft_len, draft_len), 1)
    link_mask = jnp.logical_and(parents[..., :, None] == col_ids, row_ids > 0)
    reached = jnp.logical_or(link_mask, row_ids == col_ids).astype(jnp.bfloat16)
    for doubling in range(max(1, (draft_len - 1).bit_length())):
        reached = (
            jnp.einsum("...ts,...su->...tu", reached, reached, preferred_element_type=jnp.float32)
            > 0.5
        ).astype(jnp.bfloat16)
    reached = reached.astype(jnp.float32)
    depths = (jnp.sum(reached, axis=-1) - 1.0).astype(jnp.int32)
    return (reached > 0.5, depths)


def rotate(vectors, cos_part, sin_part):
    half_dim = vectors.shape[-1] // 2
    front_half = vectors[..., :half_dim]
    back_half = vectors[..., half_dim:]
    return jnp.concatenate(
        [
            front_half * cos_part - back_half * sin_part,
            back_half * cos_part + front_half * sin_part,
        ],
        axis=-1,
    )


def attend_kernel(
    page_count, owners, groups_at_once, me_ref, q_ref, kv_ref, dkv_ref, first_ref, tree_ref, out_ref
):
    request = pl.program_id(0)
    head = pl.program_id(1)
    me = me_ref[0]
    draft_len = first_ref.shape[1]
    page_len = kv_ref.shape[2]
    width = kv_ref.shape[3]
    head_dim = width // 2
    rows = groups_at_once * draft_len
    contract_last = (((1,), (1,)), ((), ()))
    first = first_ref[0]
    slot = lax.broadcasted_iota(jnp.int32, (draft_len, page_len), 1)
    lane = lax.broadcasted_iota(jnp.int32, (page_len, width), 1)
    lane_draft = lax.broadcasted_iota(jnp.int32, (draft_len, width), 1)
    one = jnp.ones((), jnp.bfloat16)
    pages = [
        lax.rem(me + request * page_count + page, owners) for page in range(page_count)
    ]

    def part(step, carry):
        here = pl.ds(pl.multiple_of(step * rows, rows), rows)
        q = q_ref[0, 0, here, :]
        tree_bias = jnp.concatenate([tree_ref[0]] * groups_at_once, axis=0)
        tree_scores = (
            lax.dot_general(
                q, dkv_ref[0, 0], contract_last, preferred_element_type=jnp.float32
            )
            + tree_bias
        )
        top = jnp.max(tree_scores, axis=-1, keepdims=True)
        scores = []
        tops = None
        for page in range(page_count):
            bias = jnp.where(slot + page * page_len >= first, 0.0, hidden_score)
            found = lax.dot_general(
                q, kv_ref[pages[page], head], contract_last, preferred_element_type=jnp.float32
            ) + jnp.concatenate([bias] * groups_at_once, axis=0)
            scores.append(found)
            tops = found if tops is None else jnp.maximum(tops, found)
        top = jnp.maximum(top, jnp.max(tops, axis=-1, keepdims=True))
        weights = jnp.exp(tree_scores - top).astype(jnp.bfloat16)
        total = jnp.dot(
            weights,
            jnp.where(lane_draft < head_dim, one, dkv_ref[0, 0]),
            preferred_element_type=jnp.float32,
        )
        for page in range(page_count):
            weights = jnp.exp(scores[page] - top).astype(jnp.bfloat16)
            total = total + jnp.dot(
                weights,
                jnp.where(lane < head_dim, one, kv_ref[pages[page], head]),
                preferred_element_type=jnp.float32,
            )
        out_ref[0, 0, here, :] = (total[:, head_dim:] / total[:, :1]).astype(jnp.bfloat16)
        return carry

    lax.fori_loop(0, q_ref.shape[2] // rows, part, 0)


def attend(me, q, kv, draft_kv, first, tree_bias, page_count):
    count, kv_count, rows, width = q.shape
    owners = kv.shape[0]
    draft_len = first.shape[1]
    slots = page_count * kv.shape[2] + draft_len
    groups_at_once = math.gcd(rows // draft_len, 4)
    return pl.pallas_call(
        functools.partial(attend_kernel, page_count, owners, groups_at_once),
        grid=(count, kv_count),
        in_specs=[
            pl.BlockSpec(memory_space=pltpu.SMEM),
            pl.BlockSpec((1, 1, rows, width), lambda r, c: (r, c, 0, 0)),
            pl.BlockSpec(kv.shape, lambda r, c: (0, 0, 0, 0)),
            pl.BlockSpec((1, 1, draft_len, width), lambda r, c: (r, c, 0, 0)),
            pl.BlockSpec((1, draft_len, 1), lambda r, c: (r, 0, 0)),
            pl.BlockSpec((1, draft_len, draft_len), lambda r, c: (r, 0, 0)),
        ],
        out_specs=pl.BlockSpec((1, 1, rows, width // 2), lambda r, c: (r, c, 0, 0)),
        out_shape=jax.ShapeDtypeStruct((count, kv_count, rows, width // 2), jnp.bfloat16),
        compiler_params=pltpu.CompilerParams(vmem_limit_bytes=32 * 1024 * 1024),
        cost_estimate=pl.CostEstimate(
            flops=count * kv_count * rows * slots * width * 4,
            bytes_accessed=kv.size * 2 + q.size * 4,
            transcendentals=count * kv_count * rows * slots,
        ),
    )(me, q, kv, draft_kv, first, tree_bias)


def per_device(
    hidden, norm_gain, w_query, w_keyval, w_out, kv_pool, cache_len, draft_count, parents
):
    req_dev = cache_len.shape[0]
    draft_len = parents.shape[1]
    d_model = hidden.shape[2]
    head_dim = w_keyval.shape[2] // 2
    heads_here = w_query.shape[1] // head_dim
    kv_count = max(1, heads_here // (HQ // KVH))
    group_size = heads_here // kv_count
    my_tp = lax.axis_index("tp")
    kv_first = my_tp * heads_here // (HQ // KVH)
    page_len = kv_pool.shape[1]
    page_count = W // page_len
    owners = lax.axis_size("req")
    capacity = req_dev * page_count // owners
    chunk_req = owners // page_count
    me = lax.axis_index("req").astype(jnp.int32).reshape(1)
    query_width = heads_here * head_dim
    tp = lax.axis_size("tp")
    pair = tp == 2
    swap = [(0, 1), (1, 0)]

    local_pool = kv_pool.reshape((owners, capacity) + kv_pool.shape[1:])
    windows = []
    for copy in range(capacity):
        pages = lax.dynamic_slice_in_dim(local_pool[:, copy], kv_first, kv_count, 2)
        pages = pages.transpose(0, 2, 1, 3)
        windows.append(lax.all_to_all(pages, "req", split_axis=0, concat_axis=0, tiled=True))

    w_kv_mine = lax.dynamic_slice_in_dim(w_keyval, kv_first, kv_count, 1).reshape(
        d_model, kv_count * 2 * head_dim
    )
    w_both = jnp.concatenate([w_query, w_kv_mine], axis=1)
    if pair:
        inputs = jnp.concatenate([hidden, lax.ppermute(hidden, "tp", swap)], axis=0)
    else:
        inputs = lax.all_gather(hidden, "tp", axis=0, tiled=True)
    inputs = inputs.astype(jnp.float32)

    def held(entries, axis):
        if not pair:
            return entries
        return jnp.where(my_tp == 0, entries, jnp.roll(entries, draft_len // 2, axis))

    normed = (
        inputs * lax.rsqrt(jnp.mean(inputs * inputs, axis=-1, keepdims=True) + eps) * norm_gain
    ).astype(jnp.bfloat16)
    projected = jnp.einsum("trd,de->tre", normed, w_both, preferred_element_type=jnp.float32)
    reached, depths = ancestry(parents)
    reached = held(held(reached, 1), 2)
    depths = held(depths, 1)
    position = (cache_len[:, None] + depths).T
    frequency = jnp.exp(
        jnp.arange(head_dim // 2, dtype=jnp.float32) * (-2.0 * math.log(rope_base) / head_dim)
    )
    angles = position.astype(jnp.float32)[..., None, None] * frequency
    cos_part = jnp.cos(angles)
    sin_part = jnp.sin(angles)
    queries = rotate(
        projected[..., :query_width].reshape(draft_len, req_dev, heads_here, head_dim),
        cos_part,
        sin_part,
    )
    queries = (queries * head_dim ** (-0.5)).astype(jnp.bfloat16)
    queries = queries.reshape(draft_len, req_dev, kv_count, group_size, head_dim)
    queries = queries.transpose(1, 2, 3, 0, 4).reshape(
        req_dev, kv_count, group_size * draft_len, head_dim
    )
    queries = jnp.pad(queries, ((0, 0), (0, 0), (0, 0), (0, head_dim)))
    keyvals = projected[..., query_width:].reshape(draft_len, req_dev, kv_count, 2 * head_dim)
    draft_kv = jnp.concatenate(
        [rotate(keyvals[..., :head_dim], cos_part, sin_part), keyvals[..., head_dim:]], axis=-1
    ).astype(jnp.bfloat16)
    draft_kv = draft_kv.transpose(1, 2, 0, 3)
    tree_bias = jnp.where(reached, 0.0, hidden_score)
    first_slot = jnp.maximum(W - cache_len[:, None], depths + 1)[..., None]
    slots = held(jnp.arange(draft_len, dtype=jnp.int32), 0)
    valid_rows = slots[:, None] < draft_count[None, :]

    results = []
    for copy in range(capacity):
        here = slice(copy * chunk_req, (copy + 1) * chunk_req)
        mixed = attend(
            me,
            queries[here],
            windows[copy],
            draft_kv[here],
            first_slot[here],
            tree_bias[here],
            page_count,
        )
        mixed = mixed.reshape(chunk_req, kv_count, group_size, draft_len, head_dim)
        mixed = mixed.transpose(0, 3, 1, 2, 4).reshape(chunk_req, draft_len, query_width)
        term = jnp.einsum("rth,hd->rtd", mixed, w_out, preferred_element_type=jnp.float32)
        if pair:
            half = draft_len // 2
            other = lax.ppermute(term[:, half:].astype(jnp.bfloat16), "tp", swap)
            total = term[:, :half] + other.astype(jnp.float32)
            keep = valid_rows[:half, here].T[..., None]
            results.append(jnp.where(keep, total, 0.0).astype(jnp.bfloat16))
        else:
            keep = valid_rows[:, here].T[..., None]
            results.append(jnp.where(keep, term, 0.0).astype(jnp.bfloat16))
    result = jnp.concatenate(results, axis=0).transpose(1, 0, 2)
    if pair:
        return result
    return lax.psum_scatter(result, "tp", scatter_dimension=0, tiled=True)


def solution(mesh):
    in_specs = (
        P("tp", "req", None),
        P(),
        P(None, "tp"),
        P(),
        P("tp", None),
        P("req", None, None, None),
        P("req"),
        P("req"),
        P("req", None),
    )
    out_specs = P("tp", "req", None)
    return jax.shard_map(
        per_device, mesh=mesh, in_specs=in_specs, out_specs=out_specs, check_vma=False
    )
```

```python
import functools
import math

import jax
import jax.numpy as jnp
from jax import lax
from jax.experimental import pallas as pl
from jax.experimental.pallas import tpu as pltpu
from jax.sharding import PartitionSpec as P

HQ = 32
KVH = 4
W = 2048


eps = 1e-05
rope_base = 10000.0
hidden_score = -1e30


def ancestry(parents):
    draft_len = parents.shape[-1]
    row_ids = lax.broadcasted_iota(jnp.int32, (draft_len, draft_len), 0)
    col_ids = lax.broadcasted_iota(jnp.int32, (draft_len, draft_len), 1)
    link_mask = jnp.logical_and(parents[..., :, None] == col_ids, row_ids > 0)
    reached = jnp.logical_or(link_mask, row_ids == col_ids).astype(jnp.bfloat16)
    for doubling in range(max(1, (draft_len - 1).bit_length())):
        reached = (
            jnp.einsum("...ts,...su->...tu", reached, reached, preferred_element_type=jnp.float32)
            > 0.5
        ).astype(jnp.bfloat16)
    reached = reached.astype(jnp.float32)
    depths = (jnp.sum(reached, axis=-1) - 1.0).astype(jnp.int32)
    return (reached > 0.5, depths)


def rotate(vectors, cos_part, sin_part):
    half_dim = vectors.shape[-1] // 2
    front_half = vectors[..., :half_dim]
    back_half = vectors[..., half_dim:]
    return jnp.concatenate(
        [
            front_half * cos_part - back_half * sin_part,
            back_half * cos_part + front_half * sin_part,
        ],
        axis=-1,
    )


def attend_kernel(
    page_count, owners, groups_at_once, me_ref, q_ref, kv_ref, dkv_ref, first_ref, tree_ref, out_ref
):
    request = pl.program_id(0)
    head = pl.program_id(1)
    in_copy = lax.rem(request, owners // page_count)
    me = me_ref[0]
    draft_len = first_ref.shape[1]
    page_len = kv_ref.shape[3]
    width = kv_ref.shape[4]
    head_dim = width // 2
    rows = groups_at_once * draft_len
    contract_last = (((1,), (1,)), ((), ()))
    first = first_ref[0]
    slot = lax.broadcasted_iota(jnp.int32, (draft_len, page_len), 1)
    lane = lax.broadcasted_iota(jnp.int32, (page_len, width), 1)
    lane_draft = lax.broadcasted_iota(jnp.int32, (draft_len, width), 1)
    one = jnp.ones((), jnp.bfloat16)
    pages = [
        lax.rem(me + in_copy * page_count + page, owners) for page in range(page_count)
    ]

    def part(step, carry):
        here = pl.ds(pl.multiple_of(step * rows, rows), rows)
        q = q_ref[0, 0, here, :]
        tree_bias = jnp.concatenate([tree_ref[0]] * groups_at_once, axis=0)
        tree_scores = (
            lax.dot_general(
                q, dkv_ref[0, 0], contract_last, preferred_element_type=jnp.float32
            )
            + tree_bias
        )
        top = jnp.max(tree_scores, axis=-1, keepdims=True)
        scores = []
        tops = None
        for page in range(page_count):
            bias = jnp.where(slot + page * page_len >= first, 0.0, hidden_score)
            found = lax.dot_general(
                q, kv_ref[pages[page], 0, head], contract_last, preferred_element_type=jnp.float32
            ) + jnp.concatenate([bias] * groups_at_once, axis=0)
            scores.append(found)
            tops = found if tops is None else jnp.maximum(tops, found)
        top = jnp.maximum(top, jnp.max(tops, axis=-1, keepdims=True))
        weights = jnp.exp(tree_scores - top).astype(jnp.bfloat16)
        total = jnp.dot(
            weights,
            jnp.where(lane_draft < head_dim, one, dkv_ref[0, 0]),
            preferred_element_type=jnp.float32,
        )
        for page in range(page_count):
            weights = jnp.exp(scores[page] - top).astype(jnp.bfloat16)
            total = total + jnp.dot(
                weights,
                jnp.where(lane < head_dim, one, kv_ref[pages[page], 0, head]),
                preferred_element_type=jnp.float32,
            )
        mixed = (total[:, head_dim:] / total[:, :1]).astype(jnp.bfloat16)
        columns = groups_at_once * head_dim
        out_ref[0, :, pl.ds(pl.multiple_of(step * columns, columns), columns)] = jnp.concatenate(
            [mixed[g * draft_len : (g + 1) * draft_len] for g in range(groups_at_once)], axis=1
        )
        return carry

    lax.fori_loop(0, q_ref.shape[2] // rows, part, 0)


def attend(me, q, kv, draft_kv, first, tree_bias, page_count):
    count, kv_count, rows, width = q.shape
    owners = kv.shape[0]
    draft_len = first.shape[1]
    slots = page_count * kv.shape[3] + draft_len
    chunk_req = owners // page_count
    columns = rows // draft_len * (width // 2)
    groups_at_once = math.gcd(rows // draft_len, 4)
    return pl.pallas_call(
        functools.partial(attend_kernel, page_count, owners, groups_at_once),
        grid=(count, kv_count),
        in_specs=[
            pl.BlockSpec(memory_space=pltpu.SMEM),
            pl.BlockSpec((1, 1, rows, width), lambda r, c: (r, c, 0, 0)),
            pl.BlockSpec(
                (owners, 1) + kv.shape[2:], lambda r, c: (0, r // chunk_req, 0, 0, 0)
            ),
            pl.BlockSpec((1, 1, draft_len, width), lambda r, c: (r, c, 0, 0)),
            pl.BlockSpec((1, draft_len, 1), lambda r, c: (r, 0, 0)),
            pl.BlockSpec((1, draft_len, draft_len), lambda r, c: (r, 0, 0)),
        ],
        out_specs=pl.BlockSpec((1, draft_len, columns), lambda r, c: (r, 0, c)),
        out_shape=jax.ShapeDtypeStruct((count, draft_len, kv_count * columns), jnp.bfloat16),
        compiler_params=pltpu.CompilerParams(vmem_limit_bytes=32 * 1024 * 1024),
        cost_estimate=pl.CostEstimate(
            flops=count * kv_count * rows * slots * width * 4,
            bytes_accessed=kv.size * 2 + q.size * 4,
            transcendentals=count * kv_count * rows * slots,
        ),
    )(me, q, kv, draft_kv, first, tree_bias)


def per_device(
    hidden, norm_gain, w_query, w_keyval, w_out, kv_pool, cache_len, draft_count, parents
):
    req_dev = cache_len.shape[0]
    draft_len = parents.shape[1]
    d_model = hidden.shape[2]
    head_dim = w_keyval.shape[2] // 2
    heads_here = w_query.shape[1] // head_dim
    kv_count = max(1, heads_here // (HQ // KVH))
    group_size = heads_here // kv_count
    my_tp = lax.axis_index("tp")
    kv_first = my_tp * heads_here // (HQ // KVH)
    page_len = kv_pool.shape[1]
    page_count = W // page_len
    owners = lax.axis_size("req")
    capacity = req_dev * page_count // owners
    chunk_req = owners // page_count
    me = lax.axis_index("req").astype(jnp.int32).reshape(1)
    query_width = heads_here * head_dim
    tp = lax.axis_size("tp")
    pair = tp == 2
    swap = [(0, 1), (1, 0)]

    by_head = kv_pool.transpose(0, 2, 1, 3)
    by_head = by_head.reshape((owners, capacity) + by_head.shape[1:])
    cuts = [0, capacity - 1, capacity] if capacity > 1 else [0, capacity]
    spans = list(zip(cuts[:-1], cuts[1:]))
    outgoing = [
        lax.dynamic_slice(
            by_head,
            (0, start, kv_first, 0, 0),
            (owners, stop - start, kv_count) + by_head.shape[3:],
        )
        for start, stop in spans
    ]

    def exchange(pages):
        return lax.all_to_all(pages, "req", split_axis=0, concat_axis=0, tiled=True)

    first_out, hidden, w_keyval, parents, cache_len = lax.optimization_barrier(
        (outgoing[0], hidden, w_keyval, parents, cache_len)
    )
    windows = [exchange(first_out)]

    w_kv_mine = lax.dynamic_slice_in_dim(w_keyval, kv_first, kv_count, 1).reshape(
        d_model, kv_count * 2 * head_dim
    )
    w_both = jnp.concatenate([w_query, w_kv_mine], axis=1)
    if pair:
        inputs = jnp.concatenate([hidden, lax.ppermute(hidden, "tp", swap)], axis=0)
    else:
        inputs = lax.all_gather(hidden, "tp", axis=0, tiled=True)
    inputs = inputs.astype(jnp.float32)

    def held(entries, axis):
        if not pair:
            return entries
        return jnp.where(my_tp == 0, entries, jnp.roll(entries, draft_len // 2, axis))

    normed = (
        inputs * lax.rsqrt(jnp.mean(inputs * inputs, axis=-1, keepdims=True) + eps) * norm_gain
    ).astype(jnp.bfloat16)
    projected = jnp.einsum("trd,de->tre", normed, w_both, preferred_element_type=jnp.float32)
    reached, depths = ancestry(parents)
    reached = held(held(reached, 1), 2)
    depths = held(depths, 1)
    position = (cache_len[:, None] + depths).T
    frequency = jnp.exp(
        jnp.arange(head_dim // 2, dtype=jnp.float32) * (-2.0 * math.log(rope_base) / head_dim)
    )
    angles = position.astype(jnp.float32)[..., None, None] * frequency
    cos_part = jnp.cos(angles)
    sin_part = jnp.sin(angles)
    queries = rotate(
        projected[..., :query_width].reshape(draft_len, req_dev, heads_here, head_dim),
        cos_part,
        sin_part,
    )
    queries = (queries * head_dim ** (-0.5)).astype(jnp.bfloat16)
    queries = queries.reshape(draft_len, req_dev, kv_count, group_size, head_dim)
    queries = queries.transpose(1, 2, 3, 0, 4).reshape(
        req_dev, kv_count, group_size * draft_len, head_dim
    )
    queries = jnp.pad(queries, ((0, 0), (0, 0), (0, 0), (0, head_dim)))
    keyvals = projected[..., query_width:].reshape(draft_len, req_dev, kv_count, 2 * head_dim)
    draft_kv = jnp.concatenate(
        [rotate(keyvals[..., :head_dim], cos_part, sin_part), keyvals[..., head_dim:]], axis=-1
    ).astype(jnp.bfloat16)
    draft_kv = draft_kv.transpose(1, 2, 0, 3)
    tree_bias = jnp.where(reached, 0.0, hidden_score)
    first_slot = jnp.maximum(W - cache_len[:, None], depths + 1)[..., None]
    slots = held(jnp.arange(draft_len, dtype=jnp.int32), 0)
    valid_rows = slots[:, None] < draft_count[None, :]

    if len(spans) > 1:
        last, windows[0], queries, draft_kv, first_slot, tree_bias = lax.optimization_barrier(
            (outgoing[1], windows[0], queries, draft_kv, first_slot, tree_bias)
        )
        windows.append(exchange(last))

    results = []
    for window, (start, stop) in zip(windows, spans):
        here = slice(start * chunk_req, stop * chunk_req)
        mixed = attend(
            me,
            queries[here],
            window,
            draft_kv[here],
            first_slot[here],
            tree_bias[here],
            page_count,
        )
        term = jnp.einsum("rth,hd->rtd", mixed, w_out, preferred_element_type=jnp.float32)
        if pair:
            half = draft_len // 2
            other = lax.ppermute(term[:, half:].astype(jnp.bfloat16), "tp", swap)
            total = term[:, :half] + other.astype(jnp.float32)
            keep = valid_rows[:half, here].T[..., None]
            results.append(jnp.where(keep, total, 0.0).astype(jnp.bfloat16))
        else:
            keep = valid_rows[:, here].T[..., None]
            results.append(jnp.where(keep, term, 0.0).astype(jnp.bfloat16))
    result = jnp.concatenate(results, axis=0).transpose(1, 0, 2)
    if pair:
        return result
    return lax.psum_scatter(result, "tp", scatter_dimension=0, tiled=True)


def solution(mesh):
    in_specs = (
        P("tp", "req", None),
        P(),
        P(None, "tp"),
        P(),
        P("tp", None),
        P("req", None, None, None),
        P("req"),
        P("req"),
        P("req", None),
    )
    out_specs = P("tp", "req", None)
    return jax.shard_map(
        per_device, mesh=mesh, in_specs=in_specs, out_specs=out_specs, check_vma=False
    )
```

```python
import functools
import math

import jax
import jax.numpy as jnp
from jax import lax
from jax.experimental import pallas as pl
from jax.experimental.pallas import tpu as pltpu
from jax.sharding import PartitionSpec as P

HQ = 32
KVH = 4
W = 2048


eps = 1e-05
rope_base = 10000.0
hidden_score = -1e30


def ancestry(parents):
    draft_len = parents.shape[-1]
    row_ids = lax.broadcasted_iota(jnp.int32, (draft_len, draft_len), 0)
    col_ids = lax.broadcasted_iota(jnp.int32, (draft_len, draft_len), 1)
    link_mask = jnp.logical_and(parents[..., :, None] == col_ids, row_ids > 0)
    reached = jnp.logical_or(link_mask, row_ids == col_ids).astype(jnp.bfloat16)
    for doubling in range(max(1, (draft_len - 1).bit_length())):
        reached = (
            jnp.einsum("...ts,...su->...tu", reached, reached, preferred_element_type=jnp.float32)
            > 0.5
        ).astype(jnp.bfloat16)
    reached = reached.astype(jnp.float32)
    depths = (jnp.sum(reached, axis=-1) - 1.0).astype(jnp.int32)
    return (reached > 0.5, depths)


def rotate(vectors, cos_part, sin_part):
    half_dim = vectors.shape[-1] // 2
    front_half = vectors[..., :half_dim]
    back_half = vectors[..., half_dim:]
    return jnp.concatenate(
        [
            front_half * cos_part - back_half * sin_part,
            back_half * cos_part + front_half * sin_part,
        ],
        axis=-1,
    )


def attend_kernel(
    chunk_req,
    page_count,
    groups_at_once,
    pool_ref,
    near_ref,
    q_ref,
    dkv_ref,
    first_ref,
    tree_ref,
    out_ref,
    far_ref,
    send_sem,
    recv_sem,
):
    owners = near_ref.shape[0]
    later = far_ref.shape[0]
    kv_count, page_len, width = near_ref.shape[1:]
    draft_len = first_ref.shape[1]
    head_dim = width // 2
    rows = groups_at_once * draft_len
    steps = q_ref.shape[2] // rows
    columns = groups_at_once * head_dim
    contract_last = (((1,), (1,)), ((), ()))
    me = lax.axis_index("req")
    pool_heads = pool_ref.shape[2]
    heads_here = kv_count * (q_ref.shape[2] // draft_len)
    kv_first = lax.axis_index("tp") * heads_here // (HQ // pool_heads)

    def sent(copy, other):
        return pltpu.make_async_remote_copy(
            src_ref=pool_ref.at[other, copy + 1, pl.ds(kv_first, kv_count)],
            dst_ref=far_ref.at[copy, me],
            send_sem=send_sem.at[copy, other],
            recv_sem=recv_sem.at[copy, me],
            device_id={"req": other},
            device_id_type=pl.DeviceIdType.MESH,
        )

    def received(copy, other):
        return pltpu.make_async_remote_copy(
            src_ref=pool_ref.at[other, copy + 1, pl.ds(kv_first, kv_count)],
            dst_ref=far_ref.at[copy, other],
            send_sem=send_sem.at[copy, other],
            recv_sem=recv_sem.at[copy, other],
            device_id={"req": other},
            device_id_type=pl.DeviceIdType.MESH,
        )

    def kept(copy):
        return pltpu.make_async_copy(
            pool_ref.at[me, copy + 1, pl.ds(kv_first, kv_count)],
            far_ref.at[copy, me],
            recv_sem.at[copy, me],
        )

    def others(action):
        def step(offset, carry):
            action(lax.rem(me + offset, owners))
            return carry

        lax.fori_loop(1, owners, step, 0)

    barrier = pltpu.get_barrier_semaphore()
    others(
        lambda other: pl.semaphore_signal(
            barrier, inc=1, device_id={"req": other}, device_id_type=pl.DeviceIdType.MESH
        )
    )
    pl.semaphore_wait(barrier, owners - 1)
    for copy in range(later):
        others(lambda other: sent(copy, other).start())
        kept(copy).start()

    slot = lax.broadcasted_iota(jnp.int32, (draft_len, page_len), 1)
    lane = lax.broadcasted_iota(jnp.int32, (page_len, width), 1)
    lane_draft = lax.broadcasted_iota(jnp.int32, (draft_len, width), 1)
    one = jnp.ones((), jnp.bfloat16)

    def attend_copy(window, copy):
        def part(index, carry):
            step = index % steps
            head = (index // steps) % kv_count
            in_copy = index // (steps * kv_count)
            request = copy * chunk_req + in_copy
            pages = [
                lax.rem(me + in_copy * page_count + page, owners) for page in range(page_count)
            ]
            first = first_ref[request]
            draft = dkv_ref[request, head]
            q = q_ref[request, head, pl.ds(pl.multiple_of(step * rows, rows), rows), :]
            tree_scores = lax.dot_general(
                q, draft, contract_last, preferred_element_type=jnp.float32
            ) + jnp.concatenate([tree_ref[request]] * groups_at_once, axis=0)
            top = jnp.max(tree_scores, axis=-1, keepdims=True)
            scores = []
            tops = None
            for page in range(page_count):
                bias = jnp.where(slot + page * page_len >= first, 0.0, hidden_score)
                found = lax.dot_general(
                    q, window[pages[page], head], contract_last, preferred_element_type=jnp.float32
                ) + jnp.concatenate([bias] * groups_at_once, axis=0)
                scores.append(found)
                tops = found if tops is None else jnp.maximum(tops, found)
            top = jnp.maximum(top, jnp.max(tops, axis=-1, keepdims=True))
            weights = jnp.exp(tree_scores - top).astype(jnp.bfloat16)
            total = jnp.dot(
                weights,
                jnp.where(lane_draft < head_dim, one, draft),
                preferred_element_type=jnp.float32,
            )
            for page in range(page_count):
                weights = jnp.exp(scores[page] - top).astype(jnp.bfloat16)
                total = total + jnp.dot(
                    weights,
                    jnp.where(lane < head_dim, one, window[pages[page], head]),
                    preferred_element_type=jnp.float32,
                )
            mixed = (total[:, head_dim:] / total[:, :1]).astype(jnp.bfloat16)
            place = pl.multiple_of((head * steps + step) * columns, columns)
            out_ref[request, :, pl.ds(place, columns)] = jnp.concatenate(
                [mixed[g * draft_len : (g + 1) * draft_len] for g in range(groups_at_once)], axis=1
            )
            return carry

        lax.fori_loop(0, chunk_req * kv_count * steps, part, 0)

    attend_copy(near_ref, 0)

    def arrived(copy, carry):
        others(lambda other: received(copy, other).wait_recv())
        kept(copy).wait()
        attend_copy(far_ref.at[copy], copy + 1)
        return carry

    lax.fori_loop(0, later, arrived, 0)
    for copy in range(later):
        others(lambda other: sent(copy, other).wait_send())


def attend(pool, near, q, draft_kv, first, tree_bias, page_count):
    count, kv_count, rows, width = q.shape
    owners, capacity = pool.shape[:2]
    draft_len = first.shape[1]
    slots = page_count * near.shape[2] + draft_len
    groups_at_once = math.gcd(rows // draft_len, 4)
    columns = kv_count * (rows // draft_len) * (width // 2)
    vmem = pl.BlockSpec(memory_space=pltpu.VMEM)
    return pl.pallas_call(
        functools.partial(attend_kernel, owners // page_count, page_count, groups_at_once),
        in_specs=[pl.BlockSpec(memory_space=pl.ANY)] + [vmem] * 5,
        out_specs=vmem,
        out_shape=jax.ShapeDtypeStruct((count, draft_len, columns), jnp.bfloat16),
        scratch_shapes=[
            pltpu.VMEM((capacity - 1,) + near.shape, jnp.bfloat16),
            pltpu.SemaphoreType.DMA((capacity - 1, owners)),
            pltpu.SemaphoreType.DMA((capacity - 1, owners)),
        ],
        compiler_params=pltpu.CompilerParams(
            collective_id=0, has_side_effects=True, vmem_limit_bytes=36 * 1024 * 1024
        ),
        cost_estimate=pl.CostEstimate(
            flops=count * kv_count * rows * slots * width * 4,
            bytes_accessed=near.size * 2 * capacity + q.size * 4,
            transcendentals=count * kv_count * rows * slots,
        ),
    )(pool, near, q, draft_kv, first, tree_bias)


def per_device(
    hidden, norm_gain, w_query, w_keyval, w_out, kv_pool, cache_len, draft_count, parents
):
    req_dev = cache_len.shape[0]
    draft_len = parents.shape[1]
    d_model = hidden.shape[2]
    head_dim = w_keyval.shape[2] // 2
    heads_here = w_query.shape[1] // head_dim
    kv_count = max(1, heads_here // (HQ // KVH))
    group_size = heads_here // kv_count
    my_tp = lax.axis_index("tp")
    kv_first = my_tp * heads_here // (HQ // KVH)
    page_len = kv_pool.shape[1]
    page_count = W // page_len
    owners = lax.axis_size("req")
    capacity = req_dev * page_count // owners
    query_width = heads_here * head_dim
    tp = lax.axis_size("tp")
    pair = tp == 2
    swap = [(0, 1), (1, 0)]

    by_head = kv_pool.transpose(0, 2, 1, 3)
    by_head = by_head.reshape((owners, capacity) + by_head.shape[1:])
    outgoing = lax.dynamic_slice(
        by_head, (0, 0, kv_first, 0, 0), (owners, 1, kv_count) + by_head.shape[3:]
    )[:, 0]
    outgoing, hidden, w_keyval, parents, cache_len = lax.optimization_barrier(
        (outgoing, hidden, w_keyval, parents, cache_len)
    )
    near = lax.all_to_all(outgoing, "req", split_axis=0, concat_axis=0, tiled=True)

    w_kv_mine = lax.dynamic_slice_in_dim(w_keyval, kv_first, kv_count, 1).reshape(
        d_model, kv_count * 2 * head_dim
    )
    w_both = jnp.concatenate([w_query, w_kv_mine], axis=1)
    if pair:
        inputs = jnp.concatenate([hidden, lax.ppermute(hidden, "tp", swap)], axis=0)
    else:
        inputs = lax.all_gather(hidden, "tp", axis=0, tiled=True)
    inputs = inputs.astype(jnp.float32)

    def held(entries, axis):
        if not pair:
            return entries
        return jnp.where(my_tp == 0, entries, jnp.roll(entries, draft_len // 2, axis))

    normed = (
        inputs * lax.rsqrt(jnp.mean(inputs * inputs, axis=-1, keepdims=True) + eps) * norm_gain
    ).astype(jnp.bfloat16)
    projected = jnp.einsum("trd,de->tre", normed, w_both, preferred_element_type=jnp.float32)
    reached, depths = ancestry(parents)
    reached = held(held(reached, 1), 2)
    depths = held(depths, 1)
    position = (cache_len[:, None] + depths).T
    frequency = jnp.exp(
        jnp.arange(head_dim // 2, dtype=jnp.float32) * (-2.0 * math.log(rope_base) / head_dim)
    )
    angles = position.astype(jnp.float32)[..., None, None] * frequency
    cos_part = jnp.cos(angles)
    sin_part = jnp.sin(angles)
    queries = rotate(
        projected[..., :query_width].reshape(draft_len, req_dev, heads_here, head_dim),
        cos_part,
        sin_part,
    )
    queries = (queries * head_dim ** (-0.5)).astype(jnp.bfloat16)
    queries = queries.reshape(draft_len, req_dev, kv_count, group_size, head_dim)
    queries = queries.transpose(1, 2, 3, 0, 4).reshape(
        req_dev, kv_count, group_size * draft_len, head_dim
    )
    queries = jnp.pad(queries, ((0, 0), (0, 0), (0, 0), (0, head_dim)))
    keyvals = projected[..., query_width:].reshape(draft_len, req_dev, kv_count, 2 * head_dim)
    draft_kv = jnp.concatenate(
        [rotate(keyvals[..., :head_dim], cos_part, sin_part), keyvals[..., head_dim:]], axis=-1
    ).astype(jnp.bfloat16)
    draft_kv = draft_kv.transpose(1, 2, 0, 3)
    tree_bias = jnp.where(reached, 0.0, hidden_score)
    first_slot = jnp.maximum(W - cache_len[:, None], depths + 1)[..., None]
    slots = held(jnp.arange(draft_len, dtype=jnp.int32), 0)
    valid_rows = slots[:, None] < draft_count[None, :]

    mixed_all = attend(by_head, near, queries, draft_kv, first_slot, tree_bias, page_count)
    results = []
    for start in range(0, req_dev, req_dev // 2):
        here = slice(start, start + req_dev // 2)
        mixed = mixed_all[here]
        term = jnp.einsum("rth,hd->rtd", mixed, w_out, preferred_element_type=jnp.float32)
        if pair:
            half = draft_len // 2
            other = lax.ppermute(term[:, half:].astype(jnp.bfloat16), "tp", swap)
            total = term[:, :half] + other.astype(jnp.float32)
            keep = valid_rows[:half, here].T[..., None]
            results.append(jnp.where(keep, total, 0.0).astype(jnp.bfloat16))
        else:
            keep = valid_rows[:, here].T[..., None]
            results.append(jnp.where(keep, term, 0.0).astype(jnp.bfloat16))
    result = jnp.concatenate(results, axis=0).transpose(1, 0, 2)
    if pair:
        return result
    return lax.psum_scatter(result, "tp", scatter_dimension=0, tiled=True)


def solution(mesh):
    in_specs = (
        P("tp", "req", None),
        P(),
        P(None, "tp"),
        P(),
        P("tp", None),
        P("req", None, None, None),
        P("req"),
        P("req"),
        P("req", None),
    )
    out_specs = P("tp", "req", None)
    return jax.shard_map(
        per_device, mesh=mesh, in_specs=in_specs, out_specs=out_specs, check_vma=False
    )
```

```python
import functools
import math

import jax
import jax.numpy as jnp
from jax import lax
from jax.experimental import pallas as pl
from jax.experimental.pallas import tpu as pltpu
from jax.sharding import PartitionSpec as P

HQ = 32
KVH = 4
W = 2048


eps = 1e-05
rope_base = 10000.0
hidden_score = -1e30


def ancestry(parents):
    draft_len = parents.shape[-1]
    row_ids = lax.broadcasted_iota(jnp.int32, (draft_len, draft_len), 0)
    col_ids = lax.broadcasted_iota(jnp.int32, (draft_len, draft_len), 1)
    link_mask = jnp.logical_and(parents[..., :, None] == col_ids, row_ids > 0)
    reached = jnp.logical_or(link_mask, row_ids == col_ids).astype(jnp.bfloat16)
    for doubling in range(max(1, (draft_len - 1).bit_length())):
        reached = (
            jnp.einsum("...ts,...su->...tu", reached, reached, preferred_element_type=jnp.float32)
            > 0.5
        ).astype(jnp.bfloat16)
    reached = reached.astype(jnp.float32)
    depths = (jnp.sum(reached, axis=-1) - 1.0).astype(jnp.int32)
    return (reached > 0.5, depths)


def rotate(vectors, cos_part, sin_part):
    half_dim = vectors.shape[-1] // 2
    front_half = vectors[..., :half_dim]
    back_half = vectors[..., half_dim:]
    return jnp.concatenate(
        [
            front_half * cos_part - back_half * sin_part,
            back_half * cos_part + front_half * sin_part,
        ],
        axis=-1,
    )


def attend_kernel(
    page_count, owners, groups_at_once, me_ref, q_ref, kv_ref, dkv_ref, first_ref, tree_ref, out_ref
):
    request = pl.program_id(0)
    head = pl.program_id(1)
    in_copy = lax.rem(request, owners // page_count)
    me = me_ref[0]
    draft_len = first_ref.shape[1]
    page_len = kv_ref.shape[3]
    width = kv_ref.shape[4]
    head_dim = width // 2
    rows = groups_at_once * draft_len
    contract_last = (((1,), (1,)), ((), ()))
    first = first_ref[0]
    slot = lax.broadcasted_iota(jnp.int32, (draft_len, page_len), 1)
    lane = lax.broadcasted_iota(jnp.int32, (page_len, width), 1)
    lane_draft = lax.broadcasted_iota(jnp.int32, (draft_len, width), 1)
    one = jnp.ones((), jnp.bfloat16)
    pages = [
        lax.rem(me + in_copy * page_count + page, owners) for page in range(page_count)
    ]

    def part(step, carry):
        here = pl.ds(pl.multiple_of(step * rows, rows), rows)
        q = q_ref[0, 0, here, :]
        tree_bias = jnp.concatenate([tree_ref[0]] * groups_at_once, axis=0)
        tree_scores = (
            lax.dot_general(
                q, dkv_ref[0, 0], contract_last, preferred_element_type=jnp.float32
            )
            + tree_bias
        )
        top = jnp.max(tree_scores, axis=-1, keepdims=True)
        scores = []
        tops = None
        for page in range(page_count):
            bias = jnp.where(slot + page * page_len >= first, 0.0, hidden_score)
            found = lax.dot_general(
                q, kv_ref[pages[page], 0, head], contract_last, preferred_element_type=jnp.float32
            ) + jnp.concatenate([bias] * groups_at_once, axis=0)
            scores.append(found)
            tops = found if tops is None else jnp.maximum(tops, found)
        top = jnp.maximum(top, jnp.max(tops, axis=-1, keepdims=True))
        weights = jnp.exp(tree_scores - top).astype(jnp.bfloat16)
        total = jnp.dot(
            weights,
            jnp.where(lane_draft < head_dim, one, dkv_ref[0, 0]),
            preferred_element_type=jnp.float32,
        )
        for page in range(page_count):
            weights = jnp.exp(scores[page] - top).astype(jnp.bfloat16)
            total = total + jnp.dot(
                weights,
                jnp.where(lane < head_dim, one, kv_ref[pages[page], 0, head]),
                preferred_element_type=jnp.float32,
            )
        mixed = (total[:, head_dim:] / total[:, :1]).astype(jnp.bfloat16)
        columns = groups_at_once * head_dim
        out_ref[0, :, pl.ds(pl.multiple_of(step * columns, columns), columns)] = jnp.concatenate(
            [mixed[g * draft_len : (g + 1) * draft_len] for g in range(groups_at_once)], axis=1
        )
        return carry

    lax.fori_loop(0, q_ref.shape[2] // rows, part, 0)


def attend(me, q, kv, base, draft_kv, first, tree_bias, page_count):
    count, kv_count, rows, width = q.shape
    owners = kv.shape[0]
    draft_len = first.shape[1]
    slots = page_count * kv.shape[3] + draft_len
    chunk_req = owners // page_count
    columns = rows // draft_len * (width // 2)
    groups_at_once = math.gcd(rows // draft_len, 4)
    return pl.pallas_call(
        functools.partial(attend_kernel, page_count, owners, groups_at_once),
        grid=(count, kv_count),
        in_specs=[
            pl.BlockSpec(memory_space=pltpu.SMEM),
            pl.BlockSpec((1, 1, rows, width), lambda r, c: (r, c, 0, 0)),
            pl.BlockSpec(
                (owners, 1) + kv.shape[2:], lambda r, c: (0, base + r // chunk_req, 0, 0, 0)
            ),
            pl.BlockSpec((1, 1, draft_len, width), lambda r, c: (r, c, 0, 0)),
            pl.BlockSpec((1, draft_len, 1), lambda r, c: (r, 0, 0)),
            pl.BlockSpec((1, draft_len, draft_len), lambda r, c: (r, 0, 0)),
        ],
        out_specs=pl.BlockSpec((1, draft_len, columns), lambda r, c: (r, 0, c)),
        out_shape=jax.ShapeDtypeStruct((count, draft_len, kv_count * columns), jnp.bfloat16),
        compiler_params=pltpu.CompilerParams(vmem_limit_bytes=32 * 1024 * 1024),
        cost_estimate=pl.CostEstimate(
            flops=count * kv_count * rows * slots * width * 4,
            bytes_accessed=kv.size * 2 + q.size * 4,
            transcendentals=count * kv_count * rows * slots,
        ),
    )(me, q, kv, draft_kv, first, tree_bias)


def per_device(
    hidden, norm_gain, w_query, w_keyval, w_out, kv_pool, cache_len, draft_count, parents
):
    req_dev = cache_len.shape[0]
    draft_len = parents.shape[1]
    d_model = hidden.shape[2]
    head_dim = w_keyval.shape[2] // 2
    heads_here = w_query.shape[1] // head_dim
    kv_count = max(1, heads_here // (HQ // KVH))
    group_size = heads_here // kv_count
    my_tp = lax.axis_index("tp")
    kv_first = my_tp * heads_here // (HQ // KVH)
    page_len = kv_pool.shape[1]
    page_count = W // page_len
    owners = lax.axis_size("req")
    capacity = req_dev * page_count // owners
    chunk_req = owners // page_count
    me = lax.axis_index("req").astype(jnp.int32).reshape(1)
    query_width = heads_here * head_dim
    tp = lax.axis_size("tp")
    pair = tp == 2
    swap = [(0, 1), (1, 0)]

    by_head = kv_pool.transpose(0, 2, 1, 3)
    by_head = by_head.reshape((owners, capacity) + by_head.shape[1:])
    cuts = [0, capacity // 2, capacity] if capacity > 1 else [0, capacity]
    spans = list(zip(cuts[:-1], cuts[1:]))

    def outgoing(span, head):
        start, stop = span
        return lax.dynamic_slice(
            by_head,
            (0, start, head, 0, 0),
            (owners, stop - start, kv_count) + by_head.shape[3:],
        )

    def exchange(pages):
        return lax.all_to_all(pages, "req", split_axis=0, concat_axis=0, tiled=True)

    first_out, head_later, hidden, w_keyval, parents, cache_len = lax.optimization_barrier(
        (outgoing(spans[0], kv_first), kv_first, hidden, w_keyval, parents, cache_len)
    )
    windows = [exchange(first_out)]

    w_kv_mine = lax.dynamic_slice_in_dim(w_keyval, kv_first, kv_count, 1).reshape(
        d_model, kv_count * 2 * head_dim
    )
    w_both = jnp.concatenate([w_query, w_kv_mine], axis=1)
    if pair:
        inputs = jnp.concatenate([hidden, lax.ppermute(hidden, "tp", swap)], axis=0)
    else:
        inputs = lax.all_gather(hidden, "tp", axis=0, tiled=True)
    inputs = inputs.astype(jnp.float32)

    def held(entries, axis):
        if not pair:
            return entries
        return jnp.where(my_tp == 0, entries, jnp.roll(entries, draft_len // 2, axis))

    normed = (
        inputs * lax.rsqrt(jnp.mean(inputs * inputs, axis=-1, keepdims=True) + eps) * norm_gain
    ).astype(jnp.bfloat16)
    projected = jnp.einsum("trd,de->tre", normed, w_both, preferred_element_type=jnp.float32)
    reached, depths = ancestry(parents)
    reached = held(held(reached, 1), 2)
    depths = held(depths, 1)
    position = (cache_len[:, None] + depths).T
    frequency = jnp.exp(
        jnp.arange(head_dim // 2, dtype=jnp.float32) * (-2.0 * math.log(rope_base) / head_dim)
    )
    angles = position.astype(jnp.float32)[..., None, None] * frequency
    cos_part = jnp.cos(angles)
    sin_part = jnp.sin(angles)
    queries = rotate(
        projected[..., :query_width].reshape(draft_len, req_dev, heads_here, head_dim),
        cos_part,
        sin_part,
    )
    queries = (queries * head_dim ** (-0.5)).astype(jnp.bfloat16)
    queries = queries.reshape(draft_len, req_dev, kv_count, group_size, head_dim)
    queries = queries.transpose(1, 2, 3, 0, 4).reshape(
        req_dev, kv_count, group_size * draft_len, head_dim
    )
    queries = jnp.pad(queries, ((0, 0), (0, 0), (0, 0), (0, head_dim)))
    keyvals = projected[..., query_width:].reshape(draft_len, req_dev, kv_count, 2 * head_dim)
    draft_kv = jnp.concatenate(
        [rotate(keyvals[..., :head_dim], cos_part, sin_part), keyvals[..., head_dim:]], axis=-1
    ).astype(jnp.bfloat16)
    draft_kv = draft_kv.transpose(1, 2, 0, 3)
    tree_bias = jnp.where(reached, 0.0, hidden_score)
    first_slot = jnp.maximum(W - cache_len[:, None], depths + 1)[..., None]
    slots = held(jnp.arange(draft_len, dtype=jnp.int32), 0)
    valid_rows = slots[:, None] < draft_count[None, :]

    if len(spans) > 1:
        last, windows[0], queries, draft_kv, first_slot, tree_bias = lax.optimization_barrier(
            (outgoing(spans[1], head_later), windows[0], queries, draft_kv, first_slot, tree_bias)
        )
        windows.append(exchange(last))

    results = []
    parts = []
    for window, (start, stop) in zip(windows, spans):
        if start == 0:
            parts.append((window, 0, start, stop))
        else:
            parts.extend((window, copy - start, copy, copy + 1) for copy in range(start, stop))
    for window, base, start, stop in parts:
        here = slice(start * chunk_req, stop * chunk_req)
        mixed = attend(
            me,
            queries[here],
            window,
            base,
            draft_kv[here],
            first_slot[here],
            tree_bias[here],
            page_count,
        )
        term = jnp.einsum("rth,hd->rtd", mixed, w_out, preferred_element_type=jnp.float32)
        if pair:
            half = draft_len // 2
            other = lax.ppermute(term[:, half:].astype(jnp.bfloat16), "tp", swap)
            total = term[:, :half] + other.astype(jnp.float32)
            keep = valid_rows[:half, here].T[..., None]
            results.append(jnp.where(keep, total, 0.0).astype(jnp.bfloat16))
        else:
            keep = valid_rows[:, here].T[..., None]
            results.append(jnp.where(keep, term, 0.0).astype(jnp.bfloat16))
    result = jnp.concatenate(results, axis=0).transpose(1, 0, 2)
    if pair:
        return result
    return lax.psum_scatter(result, "tp", scatter_dimension=0, tiled=True)


def solution(mesh):
    in_specs = (
        P("tp", "req", None),
        P(),
        P(None, "tp"),
        P(),
        P("tp", None),
        P("req", None, None, None),
        P("req"),
        P("req"),
        P("req", None),
    )
    out_specs = P("tp", "req", None)
    return jax.shard_map(
        per_device, mesh=mesh, in_specs=in_specs, out_specs=out_specs, check_vma=False
    )
```

```python
import functools
import math

import jax
import jax.numpy as jnp
from jax import lax
from jax.experimental import pallas as pl
from jax.experimental.pallas import tpu as pltpu
from jax.sharding import PartitionSpec as P

HQ = 32
KVH = 4
W = 2048


eps = 1e-05
rope_base = 10000.0
hidden_score = -1e30


def ancestry(parents):
    draft_len = parents.shape[-1]
    row_ids = lax.broadcasted_iota(jnp.int32, (draft_len, draft_len), 0)
    col_ids = lax.broadcasted_iota(jnp.int32, (draft_len, draft_len), 1)
    link_mask = jnp.logical_and(parents[..., :, None] == col_ids, row_ids > 0)
    reached = jnp.logical_or(link_mask, row_ids == col_ids).astype(jnp.bfloat16)
    for doubling in range(max(1, (draft_len - 1).bit_length())):
        reached = (
            jnp.einsum("...ts,...su->...tu", reached, reached, preferred_element_type=jnp.float32)
            > 0.5
        ).astype(jnp.bfloat16)
    reached = reached.astype(jnp.float32)
    depths = (jnp.sum(reached, axis=-1) - 1.0).astype(jnp.int32)
    return (reached > 0.5, depths)


def rotate(vectors, cos_part, sin_part):
    half_dim = vectors.shape[-1] // 2
    front_half = vectors[..., :half_dim]
    back_half = vectors[..., half_dim:]
    return jnp.concatenate(
        [
            front_half * cos_part - back_half * sin_part,
            back_half * cos_part + front_half * sin_part,
        ],
        axis=-1,
    )


def attend_kernel(
    page_count, owners, groups_at_once, me_ref, q_ref, kv_ref, dkv_ref, first_ref, tree_ref, out_ref
):
    request = pl.program_id(0)
    head = pl.program_id(1)
    in_copy = lax.rem(request, owners // page_count)
    me = me_ref[0]
    draft_len = first_ref.shape[1]
    page_len = kv_ref.shape[3]
    width = kv_ref.shape[4]
    head_dim = width // 2
    rows = groups_at_once * draft_len
    contract_last = (((1,), (1,)), ((), ()))
    first = first_ref[0]
    slot = lax.broadcasted_iota(jnp.int32, (draft_len, page_len), 1)
    lane = lax.broadcasted_iota(jnp.int32, (page_len, width), 1)
    lane_draft = lax.broadcasted_iota(jnp.int32, (draft_len, width), 1)
    one = jnp.ones((), jnp.bfloat16)
    pages = [
        lax.rem(me + in_copy * page_count + page, owners) for page in range(page_count)
    ]

    def part(step, carry):
        here = pl.ds(pl.multiple_of(step * rows, rows), rows)
        q = q_ref[0, 0, here, :]
        tree_bias = jnp.concatenate([tree_ref[0]] * groups_at_once, axis=0)
        tree_scores = (
            lax.dot_general(
                q, dkv_ref[0, 0], contract_last, preferred_element_type=jnp.float32
            )
            + tree_bias
        )
        top = jnp.max(tree_scores, axis=-1, keepdims=True)
        scores = []
        tops = None
        for page in range(page_count):
            bias = jnp.where(slot + page * page_len >= first, 0.0, hidden_score)
            found = lax.dot_general(
                q, kv_ref[pages[page], 0, head], contract_last, preferred_element_type=jnp.float32
            ) + jnp.concatenate([bias] * groups_at_once, axis=0)
            scores.append(found)
            tops = found if tops is None else jnp.maximum(tops, found)
        top = jnp.maximum(top, jnp.max(tops, axis=-1, keepdims=True))
        weights = jnp.exp(tree_scores - top).astype(jnp.bfloat16)
        total = jnp.dot(
            weights,
            jnp.where(lane_draft < head_dim, one, dkv_ref[0, 0]),
            preferred_element_type=jnp.float32,
        )
        for page in range(page_count):
            weights = jnp.exp(scores[page] - top).astype(jnp.bfloat16)
            total = total + jnp.dot(
                weights,
                jnp.where(lane < head_dim, one, kv_ref[pages[page], 0, head]),
                preferred_element_type=jnp.float32,
            )
        mixed = (total[:, head_dim:] / total[:, :1]).astype(jnp.bfloat16)
        columns = groups_at_once * head_dim
        out_ref[0, :, pl.ds(pl.multiple_of(step * columns, columns), columns)] = jnp.concatenate(
            [mixed[g * draft_len : (g + 1) * draft_len] for g in range(groups_at_once)], axis=1
        )
        return carry

    lax.fori_loop(0, q_ref.shape[2] // rows, part, 0)


def attend(me, q, kv, draft_kv, first, tree_bias, page_count):
    count, kv_count, rows, width = q.shape
    owners = kv.shape[0]
    draft_len = first.shape[1]
    slots = page_count * kv.shape[3] + draft_len
    chunk_req = owners // page_count
    columns = rows // draft_len * (width // 2)
    groups_at_once = math.gcd(rows // draft_len, 8)
    return pl.pallas_call(
        functools.partial(attend_kernel, page_count, owners, groups_at_once),
        grid=(count, kv_count),
        in_specs=[
            pl.BlockSpec(memory_space=pltpu.SMEM),
            pl.BlockSpec((1, 1, rows, width), lambda r, c: (r, c, 0, 0)),
            pl.BlockSpec(
                (owners, 1) + kv.shape[2:], lambda r, c: (0, r // chunk_req, 0, 0, 0)
            ),
            pl.BlockSpec((1, 1, draft_len, width), lambda r, c: (r, c, 0, 0)),
            pl.BlockSpec((1, draft_len, 1), lambda r, c: (r, 0, 0)),
            pl.BlockSpec((1, draft_len, draft_len), lambda r, c: (r, 0, 0)),
        ],
        out_specs=pl.BlockSpec((1, draft_len, columns), lambda r, c: (r, 0, c)),
        out_shape=jax.ShapeDtypeStruct((count, draft_len, kv_count * columns), jnp.bfloat16),
        compiler_params=pltpu.CompilerParams(vmem_limit_bytes=32 * 1024 * 1024),
        cost_estimate=pl.CostEstimate(
            flops=count * kv_count * rows * slots * width * 4,
            bytes_accessed=kv.size * 2 + q.size * 4,
            transcendentals=count * kv_count * rows * slots,
        ),
    )(me, q, kv, draft_kv, first, tree_bias)


def per_device(
    hidden, norm_gain, w_query, w_keyval, w_out, kv_pool, cache_len, draft_count, parents
):
    req_dev = cache_len.shape[0]
    draft_len = parents.shape[1]
    d_model = hidden.shape[2]
    head_dim = w_keyval.shape[2] // 2
    heads_here = w_query.shape[1] // head_dim
    kv_count = max(1, heads_here // (HQ // KVH))
    group_size = heads_here // kv_count
    my_tp = lax.axis_index("tp")
    kv_first = my_tp * heads_here // (HQ // KVH)
    page_len = kv_pool.shape[1]
    page_count = W // page_len
    owners = lax.axis_size("req")
    capacity = req_dev * page_count // owners
    chunk_req = owners // page_count
    me = lax.axis_index("req").astype(jnp.int32).reshape(1)
    query_width = heads_here * head_dim
    tp = lax.axis_size("tp")
    pair = tp == 2
    swap = [(0, 1), (1, 0)]

    by_head = kv_pool.transpose(0, 2, 1, 3)
    by_head = by_head.reshape((owners, capacity) + by_head.shape[1:])
    cuts = [0, capacity - 1, capacity] if capacity > 1 else [0, capacity]
    spans = list(zip(cuts[:-1], cuts[1:]))
    outgoing = [
        lax.dynamic_slice(
            by_head,
            (0, start, kv_first, 0, 0),
            (owners, stop - start, kv_count) + by_head.shape[3:],
        )
        for start, stop in spans
    ]

    def exchange(pages):
        return lax.all_to_all(pages, "req", split_axis=0, concat_axis=0, tiled=True)

    first_out, hidden, w_keyval, parents, cache_len = lax.optimization_barrier(
        (outgoing[0], hidden, w_keyval, parents, cache_len)
    )
    windows = [exchange(first_out)]

    w_kv_mine = lax.dynamic_slice_in_dim(w_keyval, kv_first, kv_count, 1).reshape(
        d_model, kv_count * 2 * head_dim
    )
    w_both = jnp.concatenate([w_query, w_kv_mine], axis=1)
    if pair:
        inputs = jnp.concatenate([hidden, lax.ppermute(hidden, "tp", swap)], axis=0)
    else:
        inputs = lax.all_gather(hidden, "tp", axis=0, tiled=True)
    inputs = inputs.astype(jnp.float32)

    def held(entries, axis):
        if not pair:
            return entries
        return jnp.where(my_tp == 0, entries, jnp.roll(entries, draft_len // 2, axis))

    normed = (
        inputs * lax.rsqrt(jnp.mean(inputs * inputs, axis=-1, keepdims=True) + eps) * norm_gain
    ).astype(jnp.bfloat16)
    projected = jnp.einsum("trd,de->tre", normed, w_both, preferred_element_type=jnp.float32)
    reached, depths = ancestry(parents)
    reached = held(held(reached, 1), 2)
    depths = held(depths, 1)
    position = (cache_len[:, None] + depths).T
    frequency = jnp.exp(
        jnp.arange(head_dim // 2, dtype=jnp.float32) * (-2.0 * math.log(rope_base) / head_dim)
    )
    angles = position.astype(jnp.float32)[..., None, None] * frequency
    cos_part = jnp.cos(angles)
    sin_part = jnp.sin(angles)
    queries = rotate(
        projected[..., :query_width].reshape(draft_len, req_dev, heads_here, head_dim),
        cos_part,
        sin_part,
    )
    queries = (queries * head_dim ** (-0.5)).astype(jnp.bfloat16)
    queries = queries.reshape(draft_len, req_dev, kv_count, group_size, head_dim)
    queries = queries.transpose(1, 2, 3, 0, 4).reshape(
        req_dev, kv_count, group_size * draft_len, head_dim
    )
    queries = jnp.pad(queries, ((0, 0), (0, 0), (0, 0), (0, head_dim)))
    keyvals = projected[..., query_width:].reshape(draft_len, req_dev, kv_count, 2 * head_dim)
    draft_kv = jnp.concatenate(
        [rotate(keyvals[..., :head_dim], cos_part, sin_part), keyvals[..., head_dim:]], axis=-1
    ).astype(jnp.bfloat16)
    draft_kv = draft_kv.transpose(1, 2, 0, 3)
    tree_bias = jnp.where(reached, 0.0, hidden_score)
    first_slot = jnp.maximum(W - cache_len[:, None], depths + 1)[..., None]
    slots = held(jnp.arange(draft_len, dtype=jnp.int32), 0)
    valid_rows = slots[:, None] < draft_count[None, :]

    if len(spans) > 1:
        last, windows[0], queries, draft_kv, first_slot, tree_bias = lax.optimization_barrier(
            (outgoing[1], windows[0], queries, draft_kv, first_slot, tree_bias)
        )
        windows.append(exchange(last))

    results = []
    for window, (start, stop) in zip(windows, spans):
        here = slice(start * chunk_req, stop * chunk_req)
        mixed = attend(
            me,
            queries[here],
            window,
            draft_kv[here],
            first_slot[here],
            tree_bias[here],
            page_count,
        )
        term = jnp.einsum("rth,hd->rtd", mixed, w_out, preferred_element_type=jnp.float32)
        if pair:
            half = draft_len // 2
            other = lax.ppermute(term[:, half:].astype(jnp.bfloat16), "tp", swap)
            total = term[:, :half] + other.astype(jnp.float32)
            keep = valid_rows[:half, here].T[..., None]
            results.append(jnp.where(keep, total, 0.0).astype(jnp.bfloat16))
        else:
            keep = valid_rows[:, here].T[..., None]
            results.append(jnp.where(keep, term, 0.0).astype(jnp.bfloat16))
    result = jnp.concatenate(results, axis=0).transpose(1, 0, 2)
    if pair:
        return result
    return lax.psum_scatter(result, "tp", scatter_dimension=0, tiled=True)


def solution(mesh):
    in_specs = (
        P("tp", "req", None),
        P(),
        P(None, "tp"),
        P(),
        P("tp", None),
        P("req", None, None, None),
        P("req"),
        P("req"),
        P("req", None),
    )
    out_specs = P("tp", "req", None)
    return jax.shard_map(
        per_device, mesh=mesh, in_specs=in_specs, out_specs=out_specs, check_vma=False
    )
```
